1024 devices in a mesh: gx: 8 (over z_lo), gy: 64 (over z_hi, y, x), gz: 2 (over core).
Axes of the slice: x: 4, y: 4, z: 32 (z_hi: 4, z_lo: 8; z = z_hi * 8 + z_lo), core: 2. Of those that a mesh axis runs over, the one named last changes fastest.
Arguments:
- density: float32 [32, 512, 256], P('gx', 'gy', 'gz'), may hold values from 0.5 to 2
- velocity: float32 [3, 32, 512, 256], P(None, 'gx', 'gy', 'gz'), may hold values from -0.5 to 0.5
- magnetic: float32 [3, 32, 512, 256], P(None, 'gx', 'gy', 'gz'), may hold values from -1 to 1
- concentration: float32 [32, 512, 256], P('gx', 'gy', 'gz'), may hold values from 0 to 1
- shear_cells: int32 [2], replicated, may hold values from 0 to 511
- shear_frac: float32 [2], replicated, may hold values from 0 to 1
Outputs:
- evolved: float32 [8, 32, 512, 256], P(None, 'gx', 'gy', 'gz')
The draws below stay inside these ranges and needn't reach their ends.
All inputs are finite; a program needn't handle non-finite values.
Results may differ from the reference program's by a relative error of at most 0.0003.
Values sent between devices are 32-bit elements; how exact they have to be, the bound alone decides.
No kernel may reach another device: no remote copies, remote signals or barrier semaphores. Data moves between devices by JAX's collectives and lax.ppermute only.
A program may use at most 32 MiB of HBM per device.

```python
import math
import jax
import jax.numpy as jnp
from jax import lax

NX = 32
NY = 512
NZ = 256


def level_of(key, shape, cuts, least, top_value):
    loudness = 1.0
    for dim, parts in cuts:
        steps = jax.random.uniform(jax.random.fold_in(jax.random.fold_in(key, 6), dim), (parts,), jnp.float32, least / len(cuts), top_value / len(cuts))
        loudness = loudness * jnp.repeat(jnp.exp(steps), shape[dim] // parts).reshape((-1,) + (1,) * (len(shape) - 1 - dim))
    return loudness


def setup_inputs(seed: int = 0) -> dict:
    key_list = jax.random.split(jax.random.key(seed), 7)
    density = jnp.clip(jnp.exp(math.log(2.0) - 1.3862944 * jax.random.uniform(key_list[0], (NX, NY, NZ), jnp.float32) ** level_of(key_list[0], (NX, NY, NZ), ((0, 8), (1, 64), (2, 2)), -0.2, 0.2)), 0.5, 2.0)
    velocity = jnp.clip(jax.random.uniform(key_list[1], (3, NX, NY, NZ), jnp.float32, -0.5, 0.5) * level_of(key_list[1], (3, NX, NY, NZ), ((1, 8), (2, 64), (3, 2)), -0.4, 0.0), -0.5, 0.5)
    magnetic = jnp.clip(jax.random.uniform(key_list[2], (3, NX, NY, NZ), jnp.float32, -1.0, 1.0) * level_of(key_list[2], (3, NX, NY, NZ), ((1, 8), (2, 64), (3, 2)), -0.4, 0.0), -1.0, 1.0)
    concentration = jnp.clip(1.0 * jax.random.uniform(key_list[3], (NX, NY, NZ), jnp.float32) ** level_of(key_list[3], (NX, NY, NZ), ((0, 8), (1, 64), (2, 2)), -0.2, 0.2), 0.0, 1.0)
    shear_cells = jax.random.randint(key_list[4], (2,), 0, NY).astype(jnp.int32)
    shear_frac = jnp.clip(jax.random.uniform(key_list[5], (2,), jnp.float32, 0.0, 1.0), 0.0, 1.0)
    return {"density": density, "velocity": velocity, "magnetic": magnetic, "concentration": concentration, "shear_cells": shear_cells, "shear_frac": shear_frac}


SOUND_SQUARED = 1.0
COURANT = 0.045
SHEAR_SPEED = 1.0

def minmod_slopes(backward, forward):
    return jnp.where(backward * forward > 0.0, jnp.sign(backward) * jnp.minimum(jnp.abs(backward), jnp.abs(forward)), 0.0)

def physical_flux(conserved, normal):
    density = conserved[0]
    momentum = conserved[1:4]
    magnetic = conserved[4:7]
    velocity = momentum / density
    normal_vel = velocity[normal]
    normal_mag = magnetic[normal]
    magnetic_sq = lax.optimization_barrier(jnp.sum(magnetic * magnetic, axis=0))
    total_press = SOUND_SQUARED * density + 0.5 * magnetic_sq
    momentum_flux = momentum * normal_vel - magnetic * normal_mag
    momentum_flux = momentum_flux.at[normal].add(total_press)
    magnetic_flux = magnetic * normal_vel - velocity * normal_mag
    fluxes = jnp.concatenate([momentum[normal][None], momentum_flux, magnetic_flux, (conserved[7] * normal_vel)[None]], axis=0)
    speeds = jnp.abs(normal_vel) + jnp.sqrt(SOUND_SQUARED + magnetic_sq / density)
    return (fluxes, speeds)

def cell_range(padded, offset, length, axis_dim):
    return lax.slice_in_dim(padded, offset, offset + length, axis=axis_dim)

def flux_difference(padded, axis_dim, normal):
    inner_count = padded.shape[axis_dim] - 4
    center = cell_range(padded, 1, inner_count + 2, axis_dim)
    slopes = minmod_slopes(center - cell_range(padded, 0, inner_count + 2, axis_dim), cell_range(padded, 2, inner_count + 2, axis_dim) - center)
    upper_face = center + 0.5 * slopes
    lower_face = center - 0.5 * slopes
    left_state = cell_range(upper_face, 0, inner_count + 1, axis_dim)
    right_state = cell_range(lower_face, 1, inner_count + 1, axis_dim)
    left_flux, left_speed = physical_flux(left_state, normal)
    right_flux, right_speed = physical_flux(right_state, normal)
    fluxes = 0.5 * (left_flux + right_flux) - 0.5 * jnp.maximum(left_speed, right_speed) * (right_state - left_state)
    return cell_range(fluxes, 1, inner_count, axis_dim) - cell_range(fluxes, 0, inner_count, axis_dim)

def lagrange_weights(fraction):
    node_list = (-1, 0, 1, 2)
    weights = []
    for target in node_list:
        weight = jnp.ones((), fraction.dtype)
        for source in node_list:
            if source != target:
                weight = weight * (source - fraction) / (source - target)
        weights.append(weight)
    return weights

def section_rate(conserved, shift_cells, fraction):
    weights = lagrange_weights(fraction)
    inner_source = conserved[:, :2]
    outer_source = conserved[:, -2:]
    inner_ghost = jnp.zeros_like(inner_source)
    outer_ghost = jnp.zeros_like(outer_source)
    for position, offset in enumerate((-1, 0, 1, 2)):
        inner_ghost = inner_ghost + weights[position] * jnp.roll(outer_source, shift_cells + offset, axis=2)
        outer_ghost = outer_ghost + weights[position] * jnp.roll(inner_source, -(shift_cells + offset), axis=2)
    inner_ghost = inner_ghost.at[2].add(SHEAR_SPEED * inner_ghost[0])
    outer_ghost = outer_ghost.at[2].add(-SHEAR_SPEED * outer_ghost[0])
    radial_pad = jnp.concatenate([inner_ghost, conserved, outer_ghost], axis=1)
    azimuthal_pad = jnp.concatenate([conserved[:, :, -2:], conserved, conserved[:, :, :2]], axis=2)
    vertical_pad = jnp.concatenate([conserved[:, :, :, -2:], conserved, conserved[:, :, :, :2]], axis=3)
    radial = flux_difference(radial_pad, 1, 0)
    azimuthal = flux_difference(azimuthal_pad, 2, 1)
    vertical = flux_difference(vertical_pad, 3, 2)
    return -(radial + azimuthal + vertical)

def reference(density, velocity, magnetic, concentration, shear_cells, shear_frac):
    initial = jnp.concatenate([density[None], density[None] * velocity, magnetic, (density * concentration)[None]], axis=0)
    midway = initial + COURANT * section_rate(initial, shear_cells[0], shear_frac[0])
    return 0.5 * initial + 0.5 * (midway + COURANT * section_rate(midway, shear_cells[1], shear_frac[1]))
```

```python
import jax
import jax.numpy as jnp
from jax import lax
from jax.sharding import PartitionSpec as P

SOUND_SQUARED = 1.0
COURANT = 0.045
SHEAR_SPEED = 1.0


def minmod_slopes(backward, forward):
    return jnp.where(
        backward * forward > 0.0,
        jnp.sign(backward) * jnp.minimum(jnp.abs(backward), jnp.abs(forward)),
        0.0,
    )


def physical_flux(conserved, normal):
    density = conserved[0]
    momentum = conserved[1:4]
    magnetic = conserved[4:7]
    velocity = momentum / density
    normal_vel = velocity[normal]
    normal_mag = magnetic[normal]
    magnetic_sq = jnp.sum(magnetic * magnetic, axis=0)
    total_press = SOUND_SQUARED * density + 0.5 * magnetic_sq
    momentum_flux = momentum * normal_vel - magnetic * normal_mag
    momentum_flux = momentum_flux.at[normal].add(total_press)
    magnetic_flux = magnetic * normal_vel - velocity * normal_mag
    fluxes = jnp.concatenate(
        [momentum[normal][None], momentum_flux, magnetic_flux, (conserved[7] * normal_vel)[None]],
        axis=0,
    )
    speeds = jnp.abs(normal_vel) + jnp.sqrt(SOUND_SQUARED + magnetic_sq / density)
    return (fluxes, speeds)


def cell_range(padded, offset, length, axis_dim):
    return lax.slice_in_dim(padded, offset, offset + length, axis=axis_dim)


def flux_difference(padded, axis_dim, normal):
    inner_count = padded.shape[axis_dim] - 4
    center = cell_range(padded, 1, inner_count + 2, axis_dim)
    slopes = minmod_slopes(
        center - cell_range(padded, 0, inner_count + 2, axis_dim),
        cell_range(padded, 2, inner_count + 2, axis_dim) - center,
    )
    upper_face = center + 0.5 * slopes
    lower_face = center - 0.5 * slopes
    left_state = cell_range(upper_face, 0, inner_count + 1, axis_dim)
    right_state = cell_range(lower_face, 1, inner_count + 1, axis_dim)
    left_flux, left_speed = physical_flux(left_state, normal)
    right_flux, right_speed = physical_flux(right_state, normal)
    fluxes = 0.5 * (left_flux + right_flux) - 0.5 * jnp.maximum(left_speed, right_speed) * (
        right_state - left_state
    )
    return cell_range(fluxes, 1, inner_count, axis_dim) - cell_range(
        fluxes, 0, inner_count, axis_dim
    )


def lagrange_weights(fraction):
    node_list = (-1, 0, 1, 2)
    weights = []
    for target in node_list:
        weight = jnp.ones((), fraction.dtype)
        for source in node_list:
            if source != target:
                weight = weight * (source - fraction) / (source - target)
        weights.append(weight)
    return weights


def by_offset(near):
    rows, columns = lax.axis_size("gx"), lax.axis_size("gy")
    route = []
    for j in range(columns):
        route.append(((rows - 1) * columns + j, (rows - 1) * columns + (j + near) % columns))
        route.append((j, (j - near) % columns))
    return route


def radial_routes(blocks):
    rows, columns = lax.axis_size("gx"), lax.axis_size("gy")
    up, down = [], []
    for i in range(rows - 1):
        for j in range(columns):
            up.append((i * columns + j, (i + 1) * columns + j))
            down.append(((i + 1) * columns + j, i * columns + j))
    for j in range(columns):
        up.append(((rows - 1) * columns + j, (j + blocks) % columns))
        down.append((j, (rows - 1) * columns + (j - blocks) % columns))
    return up, down


def near_exchange(near):
    def branch(operands):
        conserved, strip, pair, first_rows, last_rows = operands
        over = ("gx", "gy")
        beyond = lax.ppermute(strip, over, by_offset(near + 1))
        own = lax.ppermute(strip, over, by_offset(near)) if near else strip
        short = lax.ppermute(pair, over, by_offset(near - 1)) if near != 1 else pair
        other = lax.ppermute(conserved, "gz", [(0, 1), (1, 0)])
        peers = lax.axis_size("gy")
        upward = [(i, (i + 1) % peers) for i in range(peers)]
        before = lax.ppermute(last_rows, "gy", upward)
        after = lax.ppermute(first_rows, "gy", [(b, a) for a, b in upward])
        return beyond, own, short, other, before, after

    return branch


def far_exchange(blocks):
    def branch(operands):
        upward, downward = operands
        up, down = radial_routes(blocks)
        over = ("gx", "gy")
        return lax.ppermute(upward, over, up), lax.ppermute(downward, over, down)

    return branch


def halos(conserved, shift_cells, fraction):
    fields, layers, block_y, block_z = conserved.shape
    columns = lax.axis_size("gy")
    is_first = lax.axis_index("gx") == 0
    is_last = lax.axis_index("gx") == lax.axis_size("gx") - 1
    blocks = (shift_cells + 1) // block_y % columns
    within = (shift_cells + 1) % block_y
    group = 8
    lower, upper = conserved[:, :2], conserved[:, -2:]
    strip = jnp.where(is_first, lower, upper)
    pair = jnp.where(is_first, strip[:, :, -2:], strip[:, :, :2]).reshape(fields, 4, block_z)
    first_rows = conserved[:, :, :2].reshape(fields, 2 * layers, block_z)
    last_rows = conserved[:, :, -2:].reshape(fields, 2 * layers, block_z)
    beyond, own, short, other, before, after = lax.switch(
        blocks % group,
        [near_exchange(n) for n in range(group)],
        (conserved, strip, pair, first_rows, last_rows),
    )
    short = short.reshape(fields, 2, 2, block_z)
    before = before.reshape(fields, layers, 2, block_z)
    after = after.reshape(fields, layers, 2, block_z)
    rows = jnp.where(
        is_first,
        jnp.concatenate([short, own, beyond], axis=2),
        jnp.concatenate([beyond, own, short], axis=2),
    )
    start = jnp.where(is_first, within, block_y - 1 - within)
    window = lax.dynamic_slice_in_dim(rows, start, block_y + 3, axis=2)
    weights = lagrange_weights(fraction)
    ghost = jnp.zeros_like(strip)
    for position in range(4):
        factor = jnp.where(is_first, weights[position], weights[3 - position])
        ghost = ghost + factor * window[:, :, position : position + block_y]
    ghost = ghost.at[2].add(jnp.where(is_first, -SHEAR_SPEED, SHEAR_SPEED) * ghost[0])
    below, above = lax.switch(
        blocks // group,
        [far_exchange(group * n) for n in range(columns // group)],
        (jnp.where(is_last, ghost, upper), jnp.where(is_first, ghost, lower)),
    )
    return below, above, before, after, other


def section_rate(conserved, shift_cells, fraction):
    below, above, before, after, other = halos(conserved, shift_cells, fraction)
    vertical = flux_difference(
        jnp.concatenate([other[..., -2:], conserved, other[..., :2]], axis=3), 3, 2
    )
    azimuthal = flux_difference(jnp.concatenate([before, conserved, after], axis=2), 2, 1)
    radial = flux_difference(jnp.concatenate([below, conserved, above], axis=1), 1, 0)
    return -(radial + azimuthal + vertical)


def body(density, velocity, magnetic, concentration, shear_cells, shear_frac):
    initial = jnp.concatenate(
        [density[None], density[None] * velocity, magnetic, (density * concentration)[None]], axis=0
    )
    midway = initial + COURANT * section_rate(initial, shear_cells[0], shear_frac[0])
    return 0.5 * initial + 0.5 * (
        midway + COURANT * section_rate(midway, shear_cells[1], shear_frac[1])
    )


def solution(mesh):
    placed = (
        P("gx", "gy", "gz"),
        P(None, "gx", "gy", "gz"),
        P(None, "gx", "gy", "gz"),
        P("gx", "gy", "gz"),
        P(),
        P(),
    )
    return jax.shard_map(
        body, mesh=mesh, in_specs=placed, out_specs=P(None, "gx", "gy", "gz"), check_vma=False
    )
```

```python
import functools
import jax
import jax.numpy as jnp
from jax import lax
from jax.experimental import pallas as pl
from jax.experimental.pallas import tpu as pltpu
from jax.sharding import PartitionSpec as P

SOUND_SQUARED = 1.0
COURANT = 0.045
SHEAR_SPEED = 1.0
FIELDS = 8
NODES = (-1, 0, 1, 2)


def minmod_slope(backward, forward):
    smaller = jnp.where(jnp.abs(backward) < jnp.abs(forward), backward, forward)
    return jnp.where(backward * forward > 0.0, smaller, 0.0)


def physical_flux(state, normal):
    density, momentum, magnetic = state[0], state[1:4], state[4:7]
    inverse = 1.0 / density
    velocity = [m * inverse for m in momentum]
    normal_vel, normal_mag = velocity[normal], magnetic[normal]
    magnetic_sq = magnetic[0] * magnetic[0] + magnetic[1] * magnetic[1] + magnetic[2] * magnetic[2]
    momentum_flux = [m * normal_vel - b * normal_mag for m, b in zip(momentum, magnetic)]
    momentum_flux[normal] = momentum_flux[normal] + (SOUND_SQUARED * density + 0.5 * magnetic_sq)
    magnetic_flux = [b * normal_vel - v * normal_mag for b, v in zip(magnetic, velocity)]
    fluxes = [momentum[normal], *momentum_flux, *magnetic_flux, state[7] * normal_vel]
    return fluxes, jnp.abs(normal_vel) + jnp.sqrt(SOUND_SQUARED + magnetic_sq * inverse)


def face_flux(left, right, normal):
    left_flux, left_speed = physical_flux(left, normal)
    right_flux, right_speed = physical_flux(right, normal)
    half_speed = 0.5 * jnp.maximum(left_speed, right_speed)
    return [
        0.5 * (lf + rf) - half_speed * (r - l)
        for lf, rf, l, r in zip(left_flux, right_flux, left, right)
    ]


def faces_of(cells):
    lower, upper = [], []
    for back, here, ahead in zip(*cells):
        half = 0.5 * minmod_slope(here - back, ahead - here)
        lower.append(here - half)
        upper.append(here + half)
    return lower, upper


def line_difference(cells, normal):
    edges = [faces_of(cells[i - 1 : i + 2]) for i in range(1, len(cells) - 1)]
    fluxes = [face_flux(a[1], b[0], normal) for a, b in zip(edges[:-1], edges[1:])]
    return [[u - l for u, l in zip(*pair)] for pair in zip(fluxes[1:], fluxes[:-1])]


def pack_rows(block, first, ref):
    for layer in range(block.shape[1]):
        for field in range(FIELDS):
            tile = block[field, layer]
            ref[field, 2 * layer : 2 * layer + 2, :] = jnp.where(first, tile[:2], tile[-2:])


def emit_sends(state_ref, odd_ref, even_ref, layers_ref):
    even_row = lax.axis_index("gx") % 2 == 0
    even_column = lax.axis_index("gy") % 2 == 0
    state = state_ref[...]
    pack_rows(state, even_column, odd_ref)
    pack_rows(state, jnp.logical_not(even_column), even_ref)
    layers_ref[...] = jnp.where(even_row, state[:, -2:], state[:, :2])


def prepare(density, velocity, magnetic, concentration, state_ref, odd_ref, even_ref, layers_ref):
    mass = density[...]
    state_ref[0] = mass
    for i in range(3):
        state_ref[1 + i] = mass * velocity[i]
        state_ref[4 + i] = magnetic[i]
    state_ref[7] = mass * concentration[...]
    emit_sends(state_ref, odd_ref, even_ref, layers_ref)


def fill_payload(rows, state, other, payload):
    row = lax.axis_index("gx")
    low_end = (row == 0) | ((row != rows - 1) & (row % 2 == 0))
    for half, block in enumerate((state, other)):
        payload[half] = jnp.where(low_end, block[:, :2], block[:, -2:])


def pick_other(near, far, picked):
    picked[0] = near[1]
    picked[1] = far[1]


def advance(
    section, rows, columns, cores, cells_ref, frac_ref, initial, state, other,
    near, far, passed_on, odd, even, across, *out
):
    result, strip_ref = out[0], out[-1]
    row, column, core = (lax.axis_index(axis) for axis in ("gx", "gy", "gz"))
    is_first, is_last = row == 0, row == rows - 1
    is_end = is_first | is_last
    even_row, even_column, low_core = row % 2 == 0, column % 2 == 0, core == 0
    layers, block_y, block_z = state.shape[1:]

    cells = cells_ref[section]
    blocks = lax.rem(lax.div(cells + 1, block_y) + columns - 1, columns)
    within = lax.rem(cells + 1, block_y)
    odd_shift = lax.rem(blocks, cores)
    start = jnp.where(
        is_first,
        block_y * (1 - odd_shift) + block_y - 1 - within,
        block_y * odd_shift + block_y - 2 + within,
    )
    fraction = frac_ref[section]
    weights = []
    for target in NODES:
        weight, scale = 1.0, 1.0
        for source in NODES:
            if source != target:
                weight = weight * (source - fraction)
                scale = scale * (source - target)
        weights.append(weight * (1.0 / scale))
    pieces = []
    for mine, passed in ((near[0], passed_on[0]), (far[0], passed_on[1])):
        pieces.append(jnp.where(low_core, mine, passed))
        pieces.append(jnp.where(low_core, passed, mine))
    for place in range(4):
        strip_ref[:, :, block_y * place : block_y * (place + 1), :] = jnp.where(
            is_first, pieces[3 - place], pieces[place]
        )
    ghost = 0.0
    for place in range(4):
        factor = jnp.where(is_first, weights[3 - place], weights[place])
        ghost = ghost + factor * strip_ref[:, :, pl.ds(start + place, block_y), :]
    push = jnp.where(is_first, SHEAR_SPEED, -SHEAR_SPEED)
    ghost = [ghost[f] + push * ghost[0] if f == 2 else ghost[f] for f in range(FIELDS)]
    below, above = [], []
    for f in range(FIELDS):
        inner = jnp.where(is_end, ghost[f], near[0, f])
        below.append(jnp.where(even_row, inner, across[f]))
        above.append(jnp.where(even_row, across[f], inner))

    line = [[below[f][i] for f in range(FIELDS)] for i in range(2)]
    line += [[state[f, i] for f in range(FIELDS)] for i in range(layers)]
    line += [[above[f][i] for f in range(FIELDS)] for i in range(2)]
    radial = line_difference(line, 0)

    before = [jnp.where(even_column, odd[f], even[f]) for f in range(FIELDS)]
    after = [jnp.where(even_column, even[f], odd[f]) for f in range(FIELDS)]
    y_index = lax.broadcasted_iota(jnp.int32, (block_y, block_z), 0)
    z_index = lax.broadcasted_iota(jnp.int32, (block_y, block_z), 1)
    for layer in range(layers):
        here = line[2 + layer]
        shifted = {0: here}
        for s in (1, 2):
            shifted[-s] = [
                jnp.where(
                    y_index < s,
                    pltpu.roll(before[f], (block_y - 2 * layer - 2 + s) % block_y, 0),
                    pltpu.roll(here[f], s, 0),
                )
                for f in range(FIELDS)
            ]
            shifted[s] = [
                jnp.where(
                    y_index >= block_y - s,
                    pltpu.roll(after[f], (block_y - s - 2 * layer) % block_y, 0),
                    pltpu.roll(here[f], block_y - s, 0),
                )
                for f in range(FIELDS)
            ]
        azimuthal = line_difference([shifted[s] for s in range(-2, 3)], 1)[0]
        beside = [other[f, layer] for f in range(FIELDS)]
        for s in (1, 2):
            shifted[-s] = [
                jnp.where(z_index < s, pltpu.roll(beside[f], s, 1), pltpu.roll(here[f], s, 1))
                for f in range(FIELDS)
            ]
            shifted[s] = [
                jnp.where(
                    z_index >= block_z - s,
                    pltpu.roll(beside[f], block_z - s, 1),
                    pltpu.roll(here[f], block_z - s, 1),
                )
                for f in range(FIELDS)
            ]
        vertical = line_difference([shifted[s] for s in range(-2, 3)], 2)[0]
        for f in range(FIELDS):
            stepped = here[f] - COURANT * (radial[layer][f] + azimuthal[f] + vertical[f])
            if section == 1:
                stepped = 0.5 * initial[f, layer] + 0.5 * stepped
            result[f, layer] = stepped
    if section == 0:
        emit_sends(result, *out[1:4])


def swaps(pairs):
    return [(a, b) for a, b in pairs] + [(b, a) for a, b in pairs]


def sheared_route(step):
    rows, columns, cores = (lax.axis_size(axis) for axis in ("gx", "gy", "gz"))
    place = lambda i, j, c: (i * columns + j % columns) * cores + c
    pairs = []
    for j in range(columns):
        for c in range(cores):
            pairs.append((place(rows - 1, j, c), place(0, j + cores * step + c, c)))
            pairs += [(place(i, j, c), place(i + 1, j, c)) for i in range(1, rows - 2, 2)]
    return swaps(pairs)


def other_core(block):
    return lax.ppermute(block, "gz", [(0, 1), (1, 0)])


def exchange(step, steps):
    def branch(operands):
        payload, odd_rows, even_rows, even_layers = operands
        everywhere = ("gx", "gy", "gz")
        near = lax.ppermute(payload, everywhere, sheared_route(step))
        far = lax.ppermute(payload, everywhere, sheared_route((step + 1) % steps))
        columns = lax.axis_size("gy")
        odd = lax.ppermute(
            odd_rows, "gy", swaps([(i, (i + 1) % columns) for i in range(1, columns, 2)])
        )
        even = lax.ppermute(even_rows, "gy", swaps([(i, i + 1) for i in range(0, columns, 2)]))
        layers = lax.ppermute(
            even_layers, "gx", swaps([(i, i + 1) for i in range(0, lax.axis_size("gx"), 2)])
        )
        return near, far, odd, even, layers

    return branch


def body(density, velocity, magnetic, concentration, shear_cells, shear_frac):
    layers, block_y, block_z = density.shape
    rows, columns, cores = (lax.axis_size(axis) for axis in ("gx", "gy", "gz"))
    shape = lambda *dims: jax.ShapeDtypeStruct(dims, jnp.float32)
    state_shape = shape(FIELDS, layers, block_y, block_z)
    packed = shape(FIELDS, 2 * layers, block_z)
    sends = [packed, packed, shape(FIELDS, 2, block_y, block_z)]
    whole = pl.BlockSpec(memory_space=pltpu.VMEM)
    scalars = pl.BlockSpec(memory_space=pltpu.SMEM)
    initial, *messages = pl.pallas_call(
        prepare,
        out_shape=[state_shape, *sends],
        in_specs=[whole] * 4,
        out_specs=[whole] * 4,
        name="prepare",
    )(density, velocity, magnetic, concentration)
    steps = columns // cores
    state = initial
    for section in range(2):
        other = other_core(state)
        payload = pl.pallas_call(
            functools.partial(fill_payload, rows),
            out_shape=shape(2, FIELDS, 2, block_y, block_z),
            in_specs=[whole] * 2,
            out_specs=whole,
            name="payload",
        )(state, other)
        blocks = ((shear_cells[section] + 1) // block_y - 1) % columns
        near, far, *rest = lax.switch(
            blocks // cores, [exchange(n, steps) for n in range(steps)], (payload, *messages)
        )
        passed = other_core(
            pl.pallas_call(
                pick_other,
                out_shape=shape(2, FIELDS, 2, block_y, block_z),
                in_specs=[whole] * 2,
                out_specs=whole,
                name="pick",
            )(near, far)
        )
        out = [state_shape, *sends] if section == 0 else [state_shape]
        state, *messages = pl.pallas_call(
            functools.partial(advance, section, rows, columns, cores),
            out_shape=out,
            in_specs=[scalars] * 2 + [whole] * 9,
            out_specs=[whole] * len(out),
            scratch_shapes=[pltpu.VMEM((FIELDS, 2, 4 * block_y, block_z), jnp.float32)],
            compiler_params=pltpu.CompilerParams(vmem_limit_bytes=16 * 1024 * 1024),
            name="advance",
        )(shear_cells, shear_frac, initial, state, other, near, far, passed, *rest)
    return state


def solution(mesh):
    placed = (
        P("gx", "gy", "gz"),
        P(None, "gx", "gy", "gz"),
        P(None, "gx", "gy", "gz"),
        P("gx", "gy", "gz"),
        P(),
        P(),
    )
    return jax.shard_map(
        body, mesh=mesh, in_specs=placed, out_specs=P(None, "gx", "gy", "gz"), check_vma=False
    )
```

```python
import functools
import jax
import jax.numpy as jnp
from jax import lax
from jax.experimental import pallas as pl
from jax.experimental.pallas import tpu as pltpu
from jax.sharding import PartitionSpec as P

SOUND_SQUARED = 1.0
COURANT = 0.045
SHEAR_SPEED = 1.0
FIELDS = 8
NODES = (-1, 0, 1, 2)


def minmod_slope(backward, forward):
    smaller = jnp.where(jnp.abs(backward) < jnp.abs(forward), backward, forward)
    return jnp.where(backward * forward > 0.0, smaller, 0.0)


def physical_flux(state, normal):
    density, momentum, magnetic = state[0], state[1:4], state[4:7]
    inverse = 1.0 / density
    velocity = [m * inverse for m in momentum]
    normal_vel, normal_mag = velocity[normal], magnetic[normal]
    magnetic_sq = magnetic[0] * magnetic[0] + magnetic[1] * magnetic[1] + magnetic[2] * magnetic[2]
    momentum_flux = [m * normal_vel - b * normal_mag for m, b in zip(momentum, magnetic)]
    momentum_flux[normal] = momentum_flux[normal] + (SOUND_SQUARED * density + 0.5 * magnetic_sq)
    magnetic_flux = [b * normal_vel - v * normal_mag for b, v in zip(magnetic, velocity)]
    fluxes = [momentum[normal], *momentum_flux, *magnetic_flux, state[7] * normal_vel]
    return fluxes, jnp.abs(normal_vel) + jnp.sqrt(SOUND_SQUARED + magnetic_sq * inverse)


def face_flux(left, right, normal):
    left_flux, left_speed = physical_flux(left, normal)
    right_flux, right_speed = physical_flux(right, normal)
    half_speed = 0.5 * jnp.maximum(left_speed, right_speed)
    return [
        0.5 * (lf + rf) - half_speed * (r - l)
        for lf, rf, l, r in zip(left_flux, right_flux, left, right)
    ]


def faces_of(cells):
    lower, upper = [], []
    for back, here, ahead in zip(*cells):
        half = 0.5 * minmod_slope(here - back, ahead - here)
        lower.append(here - half)
        upper.append(here + half)
    return lower, upper


def line_difference(cells, normal):
    edges = [faces_of(cells[i - 1 : i + 2]) for i in range(1, len(cells) - 1)]
    fluxes = [face_flux(a[1], b[0], normal) for a, b in zip(edges[:-1], edges[1:])]
    return [[u - l for u, l in zip(*pair)] for pair in zip(fluxes[1:], fluxes[:-1])]


def pack_rows(block, first, ref):
    for layer in range(block.shape[1]):
        for field in range(FIELDS):
            tile = block[field, layer]
            ref[field, 2 * layer : 2 * layer + 2, :] = jnp.where(first, tile[:2], tile[-2:])


def emit_sends(state_ref, odd_ref, even_ref, layers_ref):
    even_row = lax.axis_index("gx") % 2 == 0
    even_column = lax.axis_index("gy") % 2 == 0
    state = state_ref[...]
    pack_rows(state, even_column, odd_ref)
    pack_rows(state, jnp.logical_not(even_column), even_ref)
    layers_ref[...] = jnp.where(even_row, state[:, -2:], state[:, :2])


def prepare(density, velocity, magnetic, concentration, state_ref, odd_ref, even_ref, layers_ref):
    mass = density[...]
    state_ref[0] = mass
    for i in range(3):
        state_ref[1 + i] = mass * velocity[i]
        state_ref[4 + i] = magnetic[i]
    state_ref[7] = mass * concentration[...]
    emit_sends(state_ref, odd_ref, even_ref, layers_ref)


def fill_payload(rows, state, other, payload):
    row = lax.axis_index("gx")
    low_end = (row == 0) | ((row != rows - 1) & (row % 2 == 0))
    for half, block in enumerate((state, other)):
        payload[half] = jnp.where(low_end, block[:, :2], block[:, -2:])


def pick_other(near, far, even, layers, picked):
    picked[0] = near[1]
    picked[1] = far[1]


def advance(
    section, rows, columns, cores, cells_ref, frac_ref, initial, state, other,
    near, far, passed_on, odd, even, across, *out
):
    result, strip_ref = out[0], out[-1]
    row, column, core = (lax.axis_index(axis) for axis in ("gx", "gy", "gz"))
    is_first, is_last = row == 0, row == rows - 1
    is_end = is_first | is_last
    even_row, even_column, low_core = row % 2 == 0, column % 2 == 0, core == 0
    layers, block_y, block_z = state.shape[1:]

    cells = cells_ref[section]
    blocks = lax.rem(lax.div(cells + 1, block_y) + columns - 1, columns)
    within = lax.rem(cells + 1, block_y)
    odd_shift = lax.rem(blocks, cores)
    start = jnp.where(
        is_first,
        block_y * (1 - odd_shift) + block_y - 1 - within,
        block_y * odd_shift + block_y - 2 + within,
    )
    fraction = frac_ref[section]
    weights = []
    for target in NODES:
        weight, scale = 1.0, 1.0
        for source in NODES:
            if source != target:
                weight = weight * (source - fraction)
                scale = scale * (source - target)
        weights.append(weight * (1.0 / scale))
    pieces = []
    for mine, passed in ((near[0], passed_on[0]), (far[0], passed_on[1])):
        pieces.append(jnp.where(low_core, mine, passed))
        pieces.append(jnp.where(low_core, passed, mine))
    for place in range(4):
        strip_ref[:, :, block_y * place : block_y * (place + 1), :] = jnp.where(
            is_first, pieces[3 - place], pieces[place]
        )
    ghost = 0.0
    for place in range(4):
        factor = jnp.where(is_first, weights[3 - place], weights[place])
        ghost = ghost + factor * strip_ref[:, :, pl.ds(start + place, block_y), :]
    push = jnp.where(is_first, SHEAR_SPEED, -SHEAR_SPEED)
    ghost = [ghost[f] + push * ghost[0] if f == 2 else ghost[f] for f in range(FIELDS)]
    below, above = [], []
    for f in range(FIELDS):
        inner = jnp.where(is_end, ghost[f], near[0, f])
        below.append(jnp.where(even_row, inner, across[f]))
        above.append(jnp.where(even_row, across[f], inner))

    line = [[below[f][i] for f in range(FIELDS)] for i in range(2)]
    line += [[state[f, i] for f in range(FIELDS)] for i in range(layers)]
    line += [[above[f][i] for f in range(FIELDS)] for i in range(2)]
    radial = line_difference(line, 0)

    before = [jnp.where(even_column, odd[f], even[f]) for f in range(FIELDS)]
    after = [jnp.where(even_column, even[f], odd[f]) for f in range(FIELDS)]
    y_index = lax.broadcasted_iota(jnp.int32, (block_y, block_z), 0)
    z_index = lax.broadcasted_iota(jnp.int32, (block_y, block_z), 1)
    for layer in range(layers):
        here = line[2 + layer]
        shifted = {0: here}
        for s in (1, 2):
            shifted[-s] = [
                jnp.where(
                    y_index < s,
                    pltpu.roll(before[f], (block_y - 2 * layer - 2 + s) % block_y, 0),
                    pltpu.roll(here[f], s, 0),
                )
                for f in range(FIELDS)
            ]
            shifted[s] = [
                jnp.where(
                    y_index >= block_y - s,
                    pltpu.roll(after[f], (block_y - s - 2 * layer) % block_y, 0),
                    pltpu.roll(here[f], block_y - s, 0),
                )
                for f in range(FIELDS)
            ]
        azimuthal = line_difference([shifted[s] for s in range(-2, 3)], 1)[0]
        beside = [other[f, layer] for f in range(FIELDS)]
        for s in (1, 2):
            shifted[-s] = [
                jnp.where(z_index < s, pltpu.roll(beside[f], s, 1), pltpu.roll(here[f], s, 1))
                for f in range(FIELDS)
            ]
            shifted[s] = [
                jnp.where(
                    z_index >= block_z - s,
                    pltpu.roll(beside[f], block_z - s, 1),
                    pltpu.roll(here[f], block_z - s, 1),
                )
                for f in range(FIELDS)
            ]
        vertical = line_difference([shifted[s] for s in range(-2, 3)], 2)[0]
        for f in range(FIELDS):
            stepped = here[f] - COURANT * (radial[layer][f] + azimuthal[f] + vertical[f])
            if section == 1:
                stepped = 0.5 * initial[f, layer] + 0.5 * stepped
            result[f, layer] = stepped
    if section == 0:
        emit_sends(result, *out[1:4])


def swaps(pairs):
    return [(a, b) for a, b in pairs] + [(b, a) for a, b in pairs]


def sheared_route(step):
    rows, columns, cores = (lax.axis_size(axis) for axis in ("gx", "gy", "gz"))
    place = lambda i, j, c: (i * columns + j % columns) * cores + c
    pairs = []
    for j in range(columns):
        for c in range(cores):
            pairs.append((place(rows - 1, j, c), place(0, j + cores * step + c, c)))
            pairs += [(place(i, j, c), place(i + 1, j, c)) for i in range(1, rows - 2, 2)]
    return swaps(pairs)


def other_core(block):
    return lax.ppermute(block, "gz", [(0, 1), (1, 0)])


def exchange(step, steps):
    def branch(operands):
        payload, odd_rows, even_rows, even_layers = operands
        everywhere = ("gx", "gy", "gz")
        near = lax.ppermute(payload, everywhere, sheared_route(step))
        far = lax.ppermute(payload, everywhere, sheared_route((step + 1) % steps))
        columns = lax.axis_size("gy")
        odd = lax.ppermute(
            odd_rows, "gy", swaps([(i, (i + 1) % columns) for i in range(1, columns, 2)])
        )
        even = lax.ppermute(even_rows, "gy", swaps([(i, i + 1) for i in range(0, columns, 2)]))
        layers = lax.ppermute(
            even_layers, "gx", swaps([(i, i + 1) for i in range(0, lax.axis_size("gx"), 2)])
        )
        picked = pl.pallas_call(
            pick_other,
            out_shape=jax.ShapeDtypeStruct(near.shape, near.dtype),
            in_specs=[pl.BlockSpec(memory_space=pltpu.VMEM)] * 2
            + [pl.BlockSpec(memory_space=pl.ANY)] * 2,
            out_specs=pl.BlockSpec(memory_space=pltpu.VMEM),
            name="pick",
        )(near, far, even, layers)
        return near, far, other_core(picked), odd, even, layers

    return branch


def body(density, velocity, magnetic, concentration, shear_cells, shear_frac):
    layers, block_y, block_z = density.shape
    rows, columns, cores = (lax.axis_size(axis) for axis in ("gx", "gy", "gz"))
    shape = lambda *dims: jax.ShapeDtypeStruct(dims, jnp.float32)
    state_shape = shape(FIELDS, layers, block_y, block_z)
    packed = shape(FIELDS, 2 * layers, block_z)
    sends = [packed, packed, shape(FIELDS, 2, block_y, block_z)]
    whole = pl.BlockSpec(memory_space=pltpu.VMEM)
    scalars = pl.BlockSpec(memory_space=pltpu.SMEM)
    initial, *messages = pl.pallas_call(
        prepare,
        out_shape=[state_shape, *sends],
        in_specs=[whole] * 4,
        out_specs=[whole] * 4,
        name="prepare",
    )(density, velocity, magnetic, concentration)
    steps = columns // cores
    state = initial
    for section in range(2):
        other = other_core(state)
        payload = pl.pallas_call(
            functools.partial(fill_payload, rows),
            out_shape=shape(2, FIELDS, 2, block_y, block_z),
            in_specs=[whole] * 2,
            out_specs=whole,
            name="payload",
        )(state, other)
        blocks = ((shear_cells[section] + 1) // block_y - 1) % columns
        received = lax.switch(
            blocks // cores, [exchange(n, steps) for n in range(steps)], (payload, *messages)
        )
        out = [state_shape, *sends] if section == 0 else [state_shape]
        state, *messages = pl.pallas_call(
            functools.partial(advance, section, rows, columns, cores),
            out_shape=out,
            in_specs=[scalars] * 2 + [whole] * 9,
            out_specs=[whole] * len(out),
            scratch_shapes=[pltpu.VMEM((FIELDS, 2, 4 * block_y, block_z), jnp.float32)],
            compiler_params=pltpu.CompilerParams(vmem_limit_bytes=16 * 1024 * 1024),
            name="advance",
        )(shear_cells, shear_frac, initial, state, other, *received)
    return state


def solution(mesh):
    placed = (
        P("gx", "gy", "gz"),
        P(None, "gx", "gy", "gz"),
        P(None, "gx", "gy", "gz"),
        P("gx", "gy", "gz"),
        P(),
        P(),
    )
    return jax.shard_map(
        body, mesh=mesh, in_specs=placed, out_specs=P(None, "gx", "gy", "gz"), check_vma=False
    )
```

```python
import functools
import jax
import jax.numpy as jnp
from jax import lax
from jax.experimental import pallas as pl
from jax.experimental.pallas import tpu as pltpu
from jax.sharding import PartitionSpec as P

SOUND_SQUARED = 1.0
COURANT = 0.045
SHEAR_SPEED = 1.0
FIELDS = 8
NODES = (-1, 0, 1, 2)


def minmod_slope(backward, forward):
    smaller = jnp.where(jnp.abs(backward) < jnp.abs(forward), backward, forward)
    return jnp.where(backward * forward > 0.0, smaller, 0.0)


def physical_flux(state, normal):
    density, momentum, magnetic = state[0], state[1:4], state[4:7]
    inverse = 1.0 / density
    velocity = [m * inverse for m in momentum]
    normal_vel, normal_mag = velocity[normal], magnetic[normal]
    magnetic_sq = magnetic[0] * magnetic[0] + magnetic[1] * magnetic[1] + magnetic[2] * magnetic[2]
    momentum_flux = [m * normal_vel - b * normal_mag for m, b in zip(momentum, magnetic)]
    momentum_flux[normal] = momentum_flux[normal] + (SOUND_SQUARED * density + 0.5 * magnetic_sq)
    magnetic_flux = [b * normal_vel - v * normal_mag for b, v in zip(magnetic, velocity)]
    fluxes = [momentum[normal], *momentum_flux, *magnetic_flux, state[7] * normal_vel]
    return fluxes, jnp.abs(normal_vel) + jnp.sqrt(SOUND_SQUARED + magnetic_sq * inverse)


def face_flux(left, right, normal):
    left_flux, left_speed = physical_flux(left, normal)
    right_flux, right_speed = physical_flux(right, normal)
    half_speed = 0.5 * jnp.maximum(left_speed, right_speed)
    return [
        0.5 * (lf + rf) - half_speed * (r - l)
        for lf, rf, l, r in zip(left_flux, right_flux, left, right)
    ]


def faces_of(cells):
    lower, upper = [], []
    for back, here, ahead in zip(*cells):
        half = 0.5 * minmod_slope(here - back, ahead - here)
        lower.append(here - half)
        upper.append(here + half)
    return lower, upper


def line_difference(cells, normal):
    edges = [faces_of(cells[i - 1 : i + 2]) for i in range(1, len(cells) - 1)]
    fluxes = [face_flux(a[1], b[0], normal) for a, b in zip(edges[:-1], edges[1:])]
    return [[u - l for u, l in zip(*pair)] for pair in zip(fluxes[1:], fluxes[:-1])]


def pack_rows(block, first, ref):
    for layer in range(block.shape[1]):
        for field in range(FIELDS):
            tile = block[field, layer]
            ref[field, 2 * layer : 2 * layer + 2, :] = jnp.where(first, tile[:2], tile[-2:])


def emit_sends(rows, state_ref, odd_ref, even_ref, layers_ref, strip_ref):
    row = lax.axis_index("gx")
    even_row = row % 2 == 0
    even_column = lax.axis_index("gy") % 2 == 0
    low_end = (row == 0) | ((row != rows - 1) & even_row)
    state = state_ref[...]
    pack_rows(state, even_column, odd_ref)
    pack_rows(state, jnp.logical_not(even_column), even_ref)
    layers_ref[...] = jnp.where(even_row, state[:, -2:], state[:, :2])
    strip_ref[...] = jnp.where(low_end, state[:, :2], state[:, -2:])


def prepare(rows, density, velocity, magnetic, concentration, state_ref, *sends):
    mass = density[...]
    state_ref[0] = mass
    for i in range(3):
        state_ref[1 + i] = mass * velocity[i]
        state_ref[4 + i] = magnetic[i]
    state_ref[7] = mass * concentration[...]
    emit_sends(rows, state_ref, *sends)


def copy_all(pairs, done):
    copies = [pltpu.make_async_copy(a, b, done.at[i]) for i, (a, b) in enumerate(pairs)]
    for copy in copies:
        copy.start()
    for copy in copies:
        copy.wait()


def join_halves(strip, other_strip, payload):
    payload[0] = strip[...]
    payload[1] = other_strip[...]


def pick_other(layers, near, far, state, picked, done):
    pairs = [(near.at[1], picked.at[0]), (far.at[1], picked.at[1])]
    for k in range(layers // 2):
        pairs.append((state.at[:, 2 * k : 2 * k + 2], picked.at[2 + k]))
    copy_all(pairs, done)


def advance(
    section, rows, columns, cores, cells_ref, frac_ref, initial, state,
    near, far, passed_on, odd, even, across, *out
):
    result, strip_ref = out[0], out[-1]
    row, column, core = (lax.axis_index(axis) for axis in ("gx", "gy", "gz"))
    is_first, is_last = row == 0, row == rows - 1
    is_end = is_first | is_last
    even_row, even_column, low_core = row % 2 == 0, column % 2 == 0, core == 0
    layers, block_y, block_z = state.shape[1:]

    cells = cells_ref[section]
    blocks = lax.rem(lax.div(cells + 1, block_y) + columns - 1, columns)
    within = lax.rem(cells + 1, block_y)
    odd_shift = lax.rem(blocks, cores)
    start = jnp.where(
        is_first,
        block_y * (1 - odd_shift) + block_y - 1 - within,
        block_y * odd_shift + block_y - 2 + within,
    )
    fraction = frac_ref[section]
    weights = []
    for target in NODES:
        weight, scale = 1.0, 1.0
        for source in NODES:
            if source != target:
                weight = weight * (source - fraction)
                scale = scale * (source - target)
        weights.append(weight * (1.0 / scale))
    pieces = []
    for mine, passed in ((near[0], passed_on[0]), (far[0], passed_on[1])):
        pieces.append(jnp.where(low_core, mine, passed))
        pieces.append(jnp.where(low_core, passed, mine))
    for place in range(4):
        strip_ref[:, :, block_y * place : block_y * (place + 1), :] = jnp.where(
            is_first, pieces[3 - place], pieces[place]
        )
    ghost = 0.0
    for place in range(4):
        factor = jnp.where(is_first, weights[3 - place], weights[place])
        ghost = ghost + factor * strip_ref[:, :, pl.ds(start + place, block_y), :]
    push = jnp.where(is_first, SHEAR_SPEED, -SHEAR_SPEED)
    ghost = [ghost[f] + push * ghost[0] if f == 2 else ghost[f] for f in range(FIELDS)]
    below, above = [], []
    for f in range(FIELDS):
        inner = jnp.where(is_end, ghost[f], near[0, f])
        below.append(jnp.where(even_row, inner, across[f]))
        above.append(jnp.where(even_row, across[f], inner))

    line = [[below[f][i] for f in range(FIELDS)] for i in range(2)]
    line += [[state[f, i] for f in range(FIELDS)] for i in range(layers)]
    line += [[above[f][i] for f in range(FIELDS)] for i in range(2)]
    radial = line_difference(line, 0)

    before = [jnp.where(even_column, odd[f], even[f]) for f in range(FIELDS)]
    after = [jnp.where(even_column, even[f], odd[f]) for f in range(FIELDS)]
    y_index = lax.broadcasted_iota(jnp.int32, (block_y, block_z), 0)
    z_index = lax.broadcasted_iota(jnp.int32, (block_y, block_z), 1)
    for layer in range(layers):
        here = line[2 + layer]
        shifted = {0: here}
        for s in (1, 2):
            shifted[-s] = [
                jnp.where(
                    y_index < s,
                    pltpu.roll(before[f], (block_y - 2 * layer - 2 + s) % block_y, 0),
                    pltpu.roll(here[f], s, 0),
                )
                for f in range(FIELDS)
            ]
            shifted[s] = [
                jnp.where(
                    y_index >= block_y - s,
                    pltpu.roll(after[f], (block_y - s - 2 * layer) % block_y, 0),
                    pltpu.roll(here[f], block_y - s, 0),
                )
                for f in range(FIELDS)
            ]
        azimuthal = line_difference([shifted[s] for s in range(-2, 3)], 1)[0]
        beside = [passed_on[2 + layer // 2, f, layer % 2] for f in range(FIELDS)]
        for s in (1, 2):
            shifted[-s] = [
                jnp.where(z_index < s, pltpu.roll(beside[f], s, 1), pltpu.roll(here[f], s, 1))
                for f in range(FIELDS)
            ]
            shifted[s] = [
                jnp.where(
                    z_index >= block_z - s,
                    pltpu.roll(beside[f], block_z - s, 1),
                    pltpu.roll(here[f], block_z - s, 1),
                )
                for f in range(FIELDS)
            ]
        vertical = line_difference([shifted[s] for s in range(-2, 3)], 2)[0]
        for f in range(FIELDS):
            stepped = here[f] - COURANT * (radial[layer][f] + azimuthal[f] + vertical[f])
            if section == 1:
                stepped = 0.5 * initial[f, layer] + 0.5 * stepped
            result[f, layer] = stepped
    if section == 0:
        emit_sends(rows, result, *out[1:5])


def swaps(pairs):
    return [(a, b) for a, b in pairs] + [(b, a) for a, b in pairs]


def sheared_route(step):
    rows, columns, cores = (lax.axis_size(axis) for axis in ("gx", "gy", "gz"))
    place = lambda i, j, c: (i * columns + j % columns) * cores + c
    pairs = []
    for j in range(columns):
        for c in range(cores):
            pairs.append((place(rows - 1, j, c), place(0, j + cores * step + c, c)))
            pairs += [(place(i, j, c), place(i + 1, j, c)) for i in range(1, rows - 2, 2)]
    return swaps(pairs)


def other_core(block):
    return lax.ppermute(block, "gz", [(0, 1), (1, 0)])


def exchange(step, steps):
    def branch(operands):
        payload, odd_rows, even_rows, even_layers = operands
        everywhere = ("gx", "gy", "gz")
        near = lax.ppermute(payload, everywhere, sheared_route(step))
        far = lax.ppermute(payload, everywhere, sheared_route((step + 1) % steps))
        columns = lax.axis_size("gy")
        odd = lax.ppermute(
            odd_rows, "gy", swaps([(i, (i + 1) % columns) for i in range(1, columns, 2)])
        )
        even = lax.ppermute(even_rows, "gy", swaps([(i, i + 1) for i in range(0, columns, 2)]))
        layers = lax.ppermute(
            even_layers, "gx", swaps([(i, i + 1) for i in range(0, lax.axis_size("gx"), 2)])
        )
        return near, far, odd, even, layers

    return branch


def body(density, velocity, magnetic, concentration, shear_cells, shear_frac):
    layers, block_y, block_z = density.shape
    rows, columns, cores = (lax.axis_size(axis) for axis in ("gx", "gy", "gz"))
    shape = lambda *dims: jax.ShapeDtypeStruct(dims, jnp.float32)
    state_shape = shape(FIELDS, layers, block_y, block_z)
    packed = shape(FIELDS, 2 * layers, block_z)
    edge = shape(FIELDS, 2, block_y, block_z)
    sends = [packed, packed, edge, edge]
    whole = pl.BlockSpec(memory_space=pltpu.VMEM)
    scalars = pl.BlockSpec(memory_space=pltpu.SMEM)
    anywhere = pl.BlockSpec(memory_space=pl.ANY)
    initial, *messages, strip = pl.pallas_call(
        functools.partial(prepare, rows),
        out_shape=[state_shape, *sends],
        in_specs=[whole] * 4,
        out_specs=[whole] * 5,
        name="prepare",
    )(density, velocity, magnetic, concentration)
    steps = columns // cores
    state = initial
    for section in range(2):
        payload = pl.pallas_call(
            join_halves,
            out_shape=shape(2, *edge.shape),
            in_specs=[whole] * 2,
            out_specs=whole,
            name="payload",
        )(strip, other_core(strip))
        blocks = ((shear_cells[section] + 1) // block_y - 1) % columns
        near, far, *rest = lax.switch(
            blocks // cores, [exchange(n, steps) for n in range(steps)], (payload, *messages)
        )
        pieces = 2 + layers // 2
        picked = pl.pallas_call(
            functools.partial(pick_other, layers),
            out_shape=shape(pieces, *edge.shape),
            in_specs=[anywhere] * 3,
            out_specs=whole,
            scratch_shapes=[pltpu.SemaphoreType.DMA((pieces,))],
            name="pick",
        )(near, far, state)
        passed = other_core(picked)
        out = [state_shape, *sends] if section == 0 else [state_shape]
        advanced = pl.pallas_call(
            functools.partial(advance, section, rows, columns, cores),
            out_shape=out,
            in_specs=[scalars] * 2 + [whole] * 8,
            out_specs=[whole] * len(out),
            scratch_shapes=[pltpu.VMEM((FIELDS, 2, 4 * block_y, block_z), jnp.float32)],
            compiler_params=pltpu.CompilerParams(vmem_limit_bytes=16 * 1024 * 1024),
            name="advance",
        )(shear_cells, shear_frac, initial, state, near, far, passed, *rest)
        if section == 0:
            state, *messages, strip = advanced
    return advanced[0]


def solution(mesh):
    placed = (
        P("gx", "gy", "gz"),
        P(None, "gx", "gy", "gz"),
        P(None, "gx", "gy", "gz"),
        P("gx", "gy", "gz"),
        P(),
        P(),
    )
    return jax.shard_map(
        body, mesh=mesh, in_specs=placed, out_specs=P(None, "gx", "gy", "gz"), check_vma=False
    )
```

```python
import functools
import jax
import jax.numpy as jnp
from jax import lax
from jax.experimental import pallas as pl
from jax.experimental.pallas import tpu as pltpu
from jax.sharding import PartitionSpec as P

SOUND_SQUARED = 1.0
COURANT = 0.045
SHEAR_SPEED = 1.0
FIELDS = 8
NODES = (-1, 0, 1, 2)


def minmod_slope(backward, forward):
    smaller = jnp.where(jnp.abs(backward) < jnp.abs(forward), backward, forward)
    return jnp.where(backward * forward > 0.0, smaller, 0.0)


def physical_flux(state, normal):
    density, momentum, magnetic = state[0], state[1:4], state[4:7]
    inverse = 1.0 / density
    velocity = [m * inverse for m in momentum]
    normal_vel, normal_mag = velocity[normal], magnetic[normal]
    magnetic_sq = magnetic[0] * magnetic[0] + magnetic[1] * magnetic[1] + magnetic[2] * magnetic[2]
    momentum_flux = [m * normal_vel - b * normal_mag for m, b in zip(momentum, magnetic)]
    momentum_flux[normal] = momentum_flux[normal] + (SOUND_SQUARED * density + 0.5 * magnetic_sq)
    magnetic_flux = [b * normal_vel - v * normal_mag for b, v in zip(magnetic, velocity)]
    fluxes = [momentum[normal], *momentum_flux, *magnetic_flux, state[7] * normal_vel]
    return fluxes, jnp.abs(normal_vel) + jnp.sqrt(SOUND_SQUARED + magnetic_sq * inverse)


def face_flux(left, right, normal):
    left_flux, left_speed = physical_flux(left, normal)
    right_flux, right_speed = physical_flux(right, normal)
    half_speed = 0.5 * jnp.maximum(left_speed, right_speed)
    return [
        0.5 * (lf + rf) - half_speed * (r - l)
        for lf, rf, l, r in zip(left_flux, right_flux, left, right)
    ]


def faces_of(cells):
    lower, upper = [], []
    for back, here, ahead in zip(*cells):
        half = 0.5 * minmod_slope(here - back, ahead - here)
        lower.append(here - half)
        upper.append(here + half)
    return lower, upper


def line_difference(cells, normal):
    edges = [faces_of(cells[i - 1 : i + 2]) for i in range(1, len(cells) - 1)]
    fluxes = [face_flux(a[1], b[0], normal) for a, b in zip(edges[:-1], edges[1:])]
    return [[u - l for u, l in zip(*pair)] for pair in zip(fluxes[1:], fluxes[:-1])]


def pack_rows(block, first, ref):
    for layer in range(block.shape[1]):
        for field in range(FIELDS):
            tile = block[field, layer]
            ref[field, 2 * layer : 2 * layer + 2, :] = jnp.where(first, tile[:2], tile[-2:])


def emit_sends(rows, state_ref, odd_ref, even_ref, layers_ref, strip_ref):
    row = lax.axis_index("gx")
    even_row = row % 2 == 0
    even_column = lax.axis_index("gy") % 2 == 0
    low_end = (row == 0) | ((row != rows - 1) & even_row)
    state = state_ref[...]
    pack_rows(state, even_column, odd_ref)
    pack_rows(state, jnp.logical_not(even_column), even_ref)
    layers_ref[...] = jnp.where(even_row, state[:, -2:], state[:, :2])
    strip_ref[...] = jnp.where(low_end, state[:, :2], state[:, -2:])


def prepare(rows, density, velocity, magnetic, concentration, state_ref, *sends):
    mass = density[...]
    state_ref[0] = mass
    for i in range(3):
        state_ref[1 + i] = mass * velocity[i]
        state_ref[4 + i] = magnetic[i]
    state_ref[7] = mass * concentration[...]
    emit_sends(rows, state_ref, *sends)


def copy_all(pairs, done):
    copies = [pltpu.make_async_copy(a, b, done.at[i]) for i, (a, b) in enumerate(pairs)]
    for copy in copies:
        copy.start()
    for copy in copies:
        copy.wait()


def join_halves(strip, other_strip, payload):
    payload[0] = strip[...]
    payload[1] = other_strip[...]


def pick_other(layers, near, far, state, picked, done):
    pairs = [(near.at[1], picked.at[0]), (far.at[1], picked.at[1])]
    for k in range(layers // 2):
        pairs.append((state.at[:, 2 * k : 2 * k + 2], picked.at[2 + k]))
    copy_all(pairs, done)


def advance(
    section, rows, columns, cores, cells_ref, frac_ref, initial, state,
    near, far, passed_on, odd, even, across, *out
):
    result, strip_ref = out[0], out[-1]
    row, column, core = (lax.axis_index(axis) for axis in ("gx", "gy", "gz"))
    is_first, is_last = row == 0, row == rows - 1
    is_end = is_first | is_last
    even_row, even_column, low_core = row % 2 == 0, column % 2 == 0, core == 0
    layers, block_y, block_z = state.shape[1:]

    cells = cells_ref[section]
    blocks = lax.rem(lax.div(cells + 1, block_y) + columns - 1, columns)
    within = lax.rem(cells + 1, block_y)
    odd_shift = lax.rem(blocks, cores)
    start = jnp.where(
        is_first,
        block_y * (1 - odd_shift) + block_y - 1 - within,
        block_y * odd_shift + block_y - 2 + within,
    )
    fraction = frac_ref[section]
    weights = []
    for target in NODES:
        weight, scale = 1.0, 1.0
        for source in NODES:
            if source != target:
                weight = weight * (source - fraction)
                scale = scale * (source - target)
        weights.append(weight * (1.0 / scale))
    pieces = []
    for mine, passed in ((near[0], passed_on[0]), (far[0], passed_on[1])):
        pieces.append(jnp.where(low_core, mine, passed))
        pieces.append(jnp.where(low_core, passed, mine))
    for place in range(4):
        strip_ref[:, :, block_y * place : block_y * (place + 1), :] = jnp.where(
            is_first, pieces[3 - place], pieces[place]
        )
    ghost = 0.0
    for place in range(4):
        factor = jnp.where(is_first, weights[3 - place], weights[place])
        ghost = ghost + factor * strip_ref[:, :, pl.ds(start + place, block_y), :]
    push = jnp.where(is_first, SHEAR_SPEED, -SHEAR_SPEED)
    ghost = [ghost[f] + push * ghost[0] if f == 2 else ghost[f] for f in range(FIELDS)]
    below, above = [], []
    for f in range(FIELDS):
        inner = jnp.where(is_end, ghost[f], near[0, f])
        below.append(jnp.where(even_row, inner, across[f]))
        above.append(jnp.where(even_row, across[f], inner))

    line = [[below[f][i] for f in range(FIELDS)] for i in range(2)]
    line += [[state[f, i] for f in range(FIELDS)] for i in range(layers)]
    line += [[above[f][i] for f in range(FIELDS)] for i in range(2)]
    radial = line_difference(line, 0)

    before = [jnp.where(even_column, odd[f], even[f]) for f in range(FIELDS)]
    after = [jnp.where(even_column, even[f], odd[f]) for f in range(FIELDS)]
    y_index = lax.broadcasted_iota(jnp.int32, (block_y, block_z), 0)
    z_index = lax.broadcasted_iota(jnp.int32, (block_y, block_z), 1)
    for layer in range(layers):
        here = line[2 + layer]
        shifted = {0: here}
        for s in (1, 2):
            shifted[-s] = [
                jnp.where(
                    y_index < s,
                    pltpu.roll(before[f], (block_y - 2 * layer - 2 + s) % block_y, 0),
                    pltpu.roll(here[f], s, 0),
                )
                for f in range(FIELDS)
            ]
            shifted[s] = [
                jnp.where(
                    y_index >= block_y - s,
                    pltpu.roll(after[f], (block_y - s - 2 * layer) % block_y, 0),
                    pltpu.roll(here[f], block_y - s, 0),
                )
                for f in range(FIELDS)
            ]
        azimuthal = line_difference([shifted[s] for s in range(-2, 3)], 1)[0]
        beside = [passed_on[2 + layer // 2, f, layer % 2] for f in range(FIELDS)]
        for s in (1, 2):
            shifted[-s] = [
                jnp.where(z_index < s, pltpu.roll(beside[f], s, 1), pltpu.roll(here[f], s, 1))
                for f in range(FIELDS)
            ]
            shifted[s] = [
                jnp.where(
                    z_index >= block_z - s,
                    pltpu.roll(beside[f], block_z - s, 1),
                    pltpu.roll(here[f], block_z - s, 1),
                )
                for f in range(FIELDS)
            ]
        vertical = line_difference([shifted[s] for s in range(-2, 3)], 2)[0]
        for f in range(FIELDS):
            stepped = here[f] - COURANT * (radial[layer][f] + azimuthal[f] + vertical[f])
            if section == 1:
                stepped = 0.5 * initial[f, layer] + 0.5 * stepped
            result[f, layer] = stepped
    if section == 0:
        emit_sends(rows, result, *out[1:5])


def swaps(pairs):
    return [(a, b) for a, b in pairs] + [(b, a) for a, b in pairs]


def sheared_route(step):
    rows, columns, cores = (lax.axis_size(axis) for axis in ("gx", "gy", "gz"))
    place = lambda i, j, c: (i * columns + j % columns) * cores + c
    pairs = []
    for j in range(columns):
        for c in range(cores):
            pairs.append((place(rows - 1, j, c), place(0, j + cores * step + c, c)))
            pairs += [(place(i, j, c), place(i + 1, j, c)) for i in range(1, rows - 2, 2)]
    return swaps(pairs)


def other_core(block):
    return lax.ppermute(block, "gz", [(0, 1), (1, 0)])


def exchange(step, steps):
    def branch(operands):
        payload, odd_rows, even_rows, even_layers = operands
        everywhere = ("gx", "gy", "gz")
        near = lax.ppermute(payload, everywhere, sheared_route(step))
        far = lax.ppermute(payload, everywhere, sheared_route((step + 1) % steps))
        columns = lax.axis_size("gy")
        odd = lax.ppermute(
            odd_rows, "gy", swaps([(i, (i + 1) % columns) for i in range(1, columns, 2)])
        )
        even = lax.ppermute(even_rows, "gy", swaps([(i, i + 1) for i in range(0, columns, 2)]))
        layers = lax.ppermute(
            even_layers, "gx", swaps([(i, i + 1) for i in range(0, lax.axis_size("gx"), 2)])
        )
        return near, far, odd, even, layers

    return branch


def body(density, velocity, magnetic, concentration, shear_cells, shear_frac):
    layers, block_y, block_z = density.shape
    rows, columns, cores = (lax.axis_size(axis) for axis in ("gx", "gy", "gz"))
    shape = lambda *dims: jax.ShapeDtypeStruct(dims, jnp.float32)
    state_shape = shape(FIELDS, layers, block_y, block_z)
    packed = shape(FIELDS, 2 * layers, block_z)
    edge = shape(FIELDS, 2, block_y, block_z)
    sends = [packed, packed, edge, edge]
    whole = pl.BlockSpec(memory_space=pltpu.VMEM)
    scalars = pl.BlockSpec(memory_space=pltpu.SMEM)
    anywhere = pl.BlockSpec(memory_space=pl.ANY)
    small = pltpu.CompilerParams(vmem_limit_bytes=4 * 1024 * 1024)
    initial, *messages, strip = pl.pallas_call(
        functools.partial(prepare, rows),
        out_shape=[state_shape, *sends],
        in_specs=[whole] * 4,
        out_specs=[whole] * 5,
        compiler_params=small,
        name="prepare",
    )(density, velocity, magnetic, concentration)
    steps = columns // cores
    state = initial
    for section in range(2):
        payload = pl.pallas_call(
            join_halves,
            out_shape=shape(2, *edge.shape),
            in_specs=[whole] * 2,
            out_specs=whole,
            compiler_params=small,
            name="payload",
        )(strip, other_core(strip))
        blocks = ((shear_cells[section] + 1) // block_y - 1) % columns
        near, far, *rest = lax.switch(
            blocks // cores, [exchange(n, steps) for n in range(steps)], (payload, *messages)
        )
        pieces = 2 + layers // 2
        picked = pl.pallas_call(
            functools.partial(pick_other, layers),
            out_shape=shape(pieces, *edge.shape),
            in_specs=[anywhere] * 3,
            out_specs=whole,
            scratch_shapes=[pltpu.SemaphoreType.DMA((pieces,))],
            compiler_params=small,
            name="pick",
        )(near, far, state)
        passed = other_core(picked)
        out = [state_shape, *sends] if section == 0 else [state_shape]
        advanced = pl.pallas_call(
            functools.partial(advance, section, rows, columns, cores),
            out_shape=out,
            in_specs=[scalars] * 2 + [whole] * 8,
            out_specs=[whole] * len(out),
            scratch_shapes=[pltpu.VMEM((FIELDS, 2, 4 * block_y, block_z), jnp.float32)],
            compiler_params=pltpu.CompilerParams(vmem_limit_bytes=8 * 1024 * 1024),
            name="advance",
        )(shear_cells, shear_frac, initial, state, near, far, passed, *rest)
        if section == 0:
            state, *messages, strip = advanced
    return advanced[0]


def solution(mesh):
    placed = (
        P("gx", "gy", "gz"),
        P(None, "gx", "gy", "gz"),
        P(None, "gx", "gy", "gz"),
        P("gx", "gy", "gz"),
        P(),
        P(),
    )
    return jax.shard_map(
        body, mesh=mesh, in_specs=placed, out_specs=P(None, "gx", "gy", "gz"), check_vma=False
    )
```

```python
import functools
import jax
import jax.numpy as jnp
from jax import lax
from jax.experimental import pallas as pl
from jax.experimental.pallas import tpu as pltpu
from jax.sharding import PartitionSpec as P

SOUND_SQUARED = 1.0
COURANT = 0.045
SHEAR_SPEED = 1.0
FIELDS = 8
NODES = (-1, 0, 1, 2)


def minmod_slope(backward, forward):
    smaller = jnp.where(jnp.abs(backward) < jnp.abs(forward), backward, forward)
    return jnp.where(backward * forward > 0.0, smaller, 0.0)


def physical_flux(state, normal):
    density, momentum, magnetic = state[0], state[1:4], state[4:7]
    inverse = 1.0 / density
    velocity = [m * inverse for m in momentum]
    normal_vel, normal_mag = velocity[normal], magnetic[normal]
    magnetic_sq = magnetic[0] * magnetic[0] + magnetic[1] * magnetic[1] + magnetic[2] * magnetic[2]
    momentum_flux = [m * normal_vel - b * normal_mag for m, b in zip(momentum, magnetic)]
    momentum_flux[normal] = momentum_flux[normal] + (SOUND_SQUARED * density + 0.5 * magnetic_sq)
    magnetic_flux = [b * normal_vel - v * normal_mag for b, v in zip(magnetic, velocity)]
    fluxes = [momentum[normal], *momentum_flux, *magnetic_flux, state[7] * normal_vel]
    return fluxes, jnp.abs(normal_vel) + jnp.sqrt(SOUND_SQUARED + magnetic_sq * inverse)


def face_flux(left, right, normal):
    left_flux, left_speed = physical_flux(left, normal)
    right_flux, right_speed = physical_flux(right, normal)
    half_speed = 0.5 * jnp.maximum(left_speed, right_speed)
    return [
        0.5 * (lf + rf) - half_speed * (r - l)
        for lf, rf, l, r in zip(left_flux, right_flux, left, right)
    ]


def faces_of(cells):
    lower, upper = [], []
    for back, here, ahead in zip(*cells):
        half = 0.5 * minmod_slope(here - back, ahead - here)
        lower.append(here - half)
        upper.append(here + half)
    return lower, upper


def line_difference(cells, normal):
    edges = [faces_of(cells[i - 1 : i + 2]) for i in range(1, len(cells) - 1)]
    fluxes = [face_flux(a[1], b[0], normal) for a, b in zip(edges[:-1], edges[1:])]
    return [[u - l for u, l in zip(*pair)] for pair in zip(fluxes[1:], fluxes[:-1])]


def pack_rows(block, first, ref):
    for layer in range(block.shape[1]):
        for field in range(FIELDS):
            tile = block[field, layer]
            ref[field, 2 * layer : 2 * layer + 2, :] = jnp.where(first, tile[:2], tile[-2:])


def emit_sends(rows, state_ref, odd_ref, even_ref, layers_ref, strip_ref):
    row = lax.axis_index("gx")
    even_row = row % 2 == 0
    even_column = lax.axis_index("gy") % 2 == 0
    low_end = (row == 0) | ((row != rows - 1) & even_row)
    state = state_ref[...]
    pack_rows(state, even_column, odd_ref)
    pack_rows(state, jnp.logical_not(even_column), even_ref)
    layers_ref[...] = jnp.where(even_row, state[:, -2:], state[:, :2])
    strip_ref[...] = jnp.where(low_end, state[:, :2], state[:, -2:])


def prepare(rows, density, velocity, magnetic, concentration, state_ref, *sends):
    mass = density[...]
    state_ref[0] = mass
    for i in range(3):
        state_ref[1 + i] = mass * velocity[i]
        state_ref[4 + i] = magnetic[i]
    state_ref[7] = mass * concentration[...]
    emit_sends(rows, state_ref, *sends)


def copy_all(pairs, done):
    copies = [pltpu.make_async_copy(a, b, done.at[i]) for i, (a, b) in enumerate(pairs)]
    for copy in copies:
        copy.start()
    for copy in copies:
        copy.wait()


def join_halves(strip, other_strip, payload):
    payload[0] = strip[...]
    payload[1] = other_strip[...]


def pick_other(layers, near, far, state, picked, done):
    pairs = [(near.at[1], picked.at[0]), (far.at[1], picked.at[1])]
    for k in range(layers // 2):
        pairs.append((state.at[:, 2 * k : 2 * k + 2], picked.at[2 + k]))
    copy_all(pairs, done)


def advance(
    section, rows, columns, cores, cells_ref, frac_ref, initial, state,
    near, far, passed_on, odd, even, across, *out
):
    result, strip_ref = out[0], out[-1]
    row, column, core = (lax.axis_index(axis) for axis in ("gx", "gy", "gz"))
    is_first, is_last = row == 0, row == rows - 1
    is_end = is_first | is_last
    even_row, even_column, low_core = row % 2 == 0, column % 2 == 0, core == 0
    layers, block_y, block_z = state.shape[1:]

    cells = cells_ref[section]
    blocks = lax.rem(lax.div(cells + 1, block_y) + columns - 1, columns)
    within = lax.rem(cells + 1, block_y)
    odd_shift = lax.rem(blocks, cores)
    start = jnp.where(
        is_first,
        block_y * (1 - odd_shift) + block_y - 1 - within,
        block_y * odd_shift + block_y - 2 + within,
    )
    fraction = frac_ref[section]
    weights = []
    for target in NODES:
        weight, scale = 1.0, 1.0
        for source in NODES:
            if source != target:
                weight = weight * (source - fraction)
                scale = scale * (source - target)
        weights.append(weight * (1.0 / scale))
    pieces = []
    for mine, passed in ((near[0], passed_on[0]), (far[0], passed_on[1])):
        pieces.append(jnp.where(low_core, mine, passed))
        pieces.append(jnp.where(low_core, passed, mine))
    for place in range(4):
        strip_ref[:, :, block_y * place : block_y * (place + 1), :] = jnp.where(
            is_first, pieces[3 - place], pieces[place]
        )
    ghost = 0.0
    for place in range(4):
        factor = jnp.where(is_first, weights[3 - place], weights[place])
        ghost = ghost + factor * strip_ref[:, :, pl.ds(start + place, block_y), :]
    push = jnp.where(is_first, SHEAR_SPEED, -SHEAR_SPEED)
    ghost = [ghost[f] + push * ghost[0] if f == 2 else ghost[f] for f in range(FIELDS)]
    below, above = [], []
    for f in range(FIELDS):
        inner = jnp.where(is_end, ghost[f], near[0, f])
        below.append(jnp.where(even_row, inner, across[f]))
        above.append(jnp.where(even_row, across[f], inner))

    line = [[below[f][i] for f in range(FIELDS)] for i in range(2)]
    line += [[state[f, i] for f in range(FIELDS)] for i in range(layers)]
    line += [[above[f][i] for f in range(FIELDS)] for i in range(2)]
    radial = line_difference(line, 0)

    before = [jnp.where(even_column, odd[f], even[f]) for f in range(FIELDS)]
    after = [jnp.where(even_column, even[f], odd[f]) for f in range(FIELDS)]
    y_index = lax.broadcasted_iota(jnp.int32, (block_y, block_z), 0)
    z_index = lax.broadcasted_iota(jnp.int32, (block_y, block_z), 1)
    for layer in range(layers):
        here = line[2 + layer]
        shifted = {0: here}
        for s in (1, 2):
            shifted[-s] = [
                jnp.where(
                    y_index < s,
                    pltpu.roll(before[f], (block_y - 2 * layer - 2 + s) % block_y, 0),
                    pltpu.roll(here[f], s, 0),
                )
                for f in range(FIELDS)
            ]
            shifted[s] = [
                jnp.where(
                    y_index >= block_y - s,
                    pltpu.roll(after[f], (block_y - s - 2 * layer) % block_y, 0),
                    pltpu.roll(here[f], block_y - s, 0),
                )
                for f in range(FIELDS)
            ]
        azimuthal = line_difference([shifted[s] for s in range(-2, 3)], 1)[0]
        beside = [passed_on[2 + layer // 2, f, layer % 2] for f in range(FIELDS)]
        for s in (1, 2):
            shifted[-s] = [
                jnp.where(z_index < s, pltpu.roll(beside[f], s, 1), pltpu.roll(here[f], s, 1))
                for f in range(FIELDS)
            ]
            shifted[s] = [
                jnp.where(
                    z_index >= block_z - s,
                    pltpu.roll(beside[f], block_z - s, 1),
                    pltpu.roll(here[f], block_z - s, 1),
                )
                for f in range(FIELDS)
            ]
        vertical = line_difference([shifted[s] for s in range(-2, 3)], 2)[0]
        for f in range(FIELDS):
            stepped = here[f] - COURANT * (radial[layer][f] + azimuthal[f] + vertical[f])
            if section == 1:
                stepped = 0.5 * initial[f, layer] + 0.5 * stepped
            result[f, layer] = stepped
    if section == 0:
        emit_sends(rows, result, *out[1:5])


def swaps(pairs):
    return [(a, b) for a, b in pairs] + [(b, a) for a, b in pairs]


def sheared_route(step):
    rows, columns, cores = (lax.axis_size(axis) for axis in ("gx", "gy", "gz"))
    place = lambda i, j, c: (i * columns + j % columns) * cores + c
    pairs = []
    for j in range(columns):
        for c in range(cores):
            pairs.append((place(rows - 1, j, c), place(0, j + cores * step + c, c)))
            pairs += [(place(i, j, c), place(i + 1, j, c)) for i in range(1, rows - 2, 2)]
    return swaps(pairs)


def other_core(block):
    return lax.ppermute(block, "gz", [(0, 1), (1, 0)])


def exchange(step, steps):
    def branch(operands):
        payload, odd_rows, even_rows, even_layers = operands
        everywhere = ("gx", "gy", "gz")
        near = lax.ppermute(payload, everywhere, sheared_route(step))
        far = lax.ppermute(payload, everywhere, sheared_route((step + 1) % steps))
        columns = lax.axis_size("gy")
        odd = lax.ppermute(
            odd_rows, "gy", swaps([(i, (i + 1) % columns) for i in range(1, columns, 2)])
        )
        even = lax.ppermute(even_rows, "gy", swaps([(i, i + 1) for i in range(0, columns, 2)]))
        layers = lax.ppermute(
            even_layers, "gx", swaps([(i, i + 1) for i in range(0, lax.axis_size("gx"), 2)])
        )
        return near, far, odd, even, layers

    return branch


def body(density, velocity, magnetic, concentration, shear_cells, shear_frac):
    layers, block_y, block_z = density.shape
    rows, columns, cores = (lax.axis_size(axis) for axis in ("gx", "gy", "gz"))
    shape = lambda *dims: jax.ShapeDtypeStruct(dims, jnp.float32)
    state_shape = shape(FIELDS, layers, block_y, block_z)
    packed = shape(FIELDS, 2 * layers, block_z)
    edge = shape(FIELDS, 2, block_y, block_z)
    sends = [packed, packed, edge, edge]
    whole = pl.BlockSpec(memory_space=pltpu.VMEM)
    scalars = pl.BlockSpec(memory_space=pltpu.SMEM)
    anywhere = pl.BlockSpec(memory_space=pl.ANY)
    small = pltpu.CompilerParams(vmem_limit_bytes=4 * 1024 * 1024)
    initial, *messages, strip = pl.pallas_call(
        functools.partial(prepare, rows),
        out_shape=[state_shape, *sends],
        in_specs=[whole] * 4,
        out_specs=[whole] * 5,
        name="prepare",
    )(density, velocity, magnetic, concentration)
    steps = columns // cores
    state = initial
    for section in range(2):
        payload = pl.pallas_call(
            join_halves,
            out_shape=shape(2, *edge.shape),
            in_specs=[whole] * 2,
            out_specs=whole,
            compiler_params=small,
            name="payload",
        )(strip, other_core(strip))
        blocks = ((shear_cells[section] + 1) // block_y - 1) % columns
        near, far, *rest = lax.switch(
            blocks // cores, [exchange(n, steps) for n in range(steps)], (payload, *messages)
        )
        pieces = 2 + layers // 2
        picked = pl.pallas_call(
            functools.partial(pick_other, layers),
            out_shape=shape(pieces, *edge.shape),
            in_specs=[anywhere] * 3,
            out_specs=whole,
            scratch_shapes=[pltpu.SemaphoreType.DMA((pieces,))],
            compiler_params=small,
            name="pick",
        )(near, far, state)
        passed = other_core(picked)
        out = [state_shape, *sends] if section == 0 else [state_shape]
        advanced = pl.pallas_call(
            functools.partial(advance, section, rows, columns, cores),
            out_shape=out,
            in_specs=[scalars] * 2 + [whole] * 8,
            out_specs=[whole] * len(out),
            scratch_shapes=[pltpu.VMEM((FIELDS, 2, 4 * block_y, block_z), jnp.float32)],
            compiler_params=pltpu.CompilerParams(vmem_limit_bytes=8 * 1024 * 1024),
            name="advance",
        )(shear_cells, shear_frac, initial, state, near, far, passed, *rest)
        if section == 0:
            state, *messages, strip = advanced
    return advanced[0]


def solution(mesh):
    placed = (
        P("gx", "gy", "gz"),
        P(None, "gx", "gy", "gz"),
        P(None, "gx", "gy", "gz"),
        P("gx", "gy", "gz"),
        P(),
        P(),
    )
    return jax.shard_map(
        body, mesh=mesh, in_specs=placed, out_specs=P(None, "gx", "gy", "gz"), check_vma=False
    )
```
